32 devices in a mesh: groups: 2 (over y), rows: 4 (over x, core), mods: 4 (over z).
Axes of the slice: x: 2, y: 2, z: 4, core: 2. Of those that a mesh axis runs over, the one named last changes fastest.
Arguments:
- query_grads: float32 [512, 16, 1024], P(('groups', 'rows'), 'mods'), parts along dimension 0, may hold values from -6 to 6
- train_grads: bfloat16 [8192, 16, 1024], P(('groups', 'rows'), 'mods'), parts along dimension 0, may hold values from -48 to 48
- token_counts: int32 [8192], P(('groups', 'rows')), parts along dimension 0, may hold values from 256 to 2048
- query_owner: int32 [512], P('groups'), parts along dimension 0, may hold values from 0 to 255, each once
- module_map: int32 [16], replicated, may hold values from 0 to 15, each once
- out_basis: float32 [16, 32, 32], replicated, may hold values from -1 to 1
- in_basis: float32 [16, 32, 32], replicated, may hold values from -1 to 1
- eigen_values: float32 [16, 1024], replicated, may hold values from 0.05 to 5
Outputs:
- scores: float32 [512, 4096], P(('groups', 'mods'), 'rows'), parts along dimension 0
The draws below stay inside these ranges and needn't reach their ends.
There are 2 independent parts, one for each index of `groups`. The reference program is written for one: setup_inputs(seed, part) draws one part's arguments, and reference() takes and returns one part's arrays. A program takes and returns all parts, laid end to end along the dimension named above; an argument that names none is the same for every part. Nothing has to cross between parts.
Inputs may be any that keep to these rules, and one draw needn't show every extreme that they name: `query_owner`: each query id stands in exactly one slot. `module_map`: each module stands in exactly one slot.
All inputs are finite; a program needn't handle non-finite values.
Results may differ from the reference program's by a relative error of at most 0.0038.
Values may be sent and summed in bfloat16 or wider, within the bound.
A program may use at most 192 MiB of HBM per device.

```python
import math
import jax
import jax.numpy as jnp
from jax import lax

FACTOR = 32
FEAT = 1024
TRAIN_DEV = 1024
QUERIES = 256
TRAIN = 4096
MODULES = 16


def set_ends(result, key, low, largest):
    longest = result.shape.index(max(result.shape))
    spots = []
    for shift in (0, 1):
        where = [jax.random.randint(jax.random.fold_in(key, axis), (), 0, length) for axis, length in enumerate(result.shape)]
        where[longest] = (where[longest] + shift) % result.shape[longest]
        spots.append(tuple(where))
    return result.at[spots[0]].set(low).at[spots[1]].set(largest)


def levels(key, shape, pieces, smallest, largest):
    loudness, own = 1.0, jax.random.fold_in(key, 6)
    for dim, blocks in pieces:
        draws = jnp.exp(jax.random.uniform(jax.random.fold_in(own, dim), (blocks,), jnp.float32, smallest / len(pieces), largest / len(pieces)))
        loudness = loudness * jnp.repeat(draws, shape[dim] // blocks).reshape([-1 if axis == dim else 1 for axis in range(len(shape))])
    return loudness


def bell_draw(rng, dims, scale, reach, shards=(), held_as=jnp.bfloat16):
    array = jax.random.normal(rng, dims, jnp.float32) * scale
    if len(shards) > 0:
        array = levels(rng, dims, shards, -0.22, 0.18) * array
    return jnp.clip(array, min=-reach, max=reach).astype(held_as)


def setup_inputs(seed: int = 0, part: int = 0) -> dict:
    keys = jax.random.split(jax.random.key(seed), 9)
    part_splits = jax.random.split(jax.random.fold_in(keys[8], part), 9)
    query_grads = bell_draw(part_splits[0], (QUERIES, MODULES, FEAT), 1.0, 6.0, ((0, 4), (1, 4)), jnp.float32)
    train_grads = bell_draw(part_splits[1], (TRAIN, MODULES, FEAT), (1024 * (MODULES * 1024) ** -0.5), 48.0, ((0, 4), (1, 4)))
    token_counts = set_ends(jax.random.randint(part_splits[2], (TRAIN,), 256, 2049), jax.random.fold_in(part_splits[2], 1), 256, 2048).astype(jnp.int32)
    query_owner = jax.random.permutation(part_splits[3], QUERIES).astype(jnp.int32)
    module_map = jax.random.permutation(keys[4], MODULES).astype(jnp.int32)
    out_basis = bell_draw(keys[5], (MODULES, FACTOR, FACTOR), FACTOR ** -0.5, 1.0, (), jnp.float32)
    in_basis = bell_draw(keys[6], (MODULES, FACTOR, FACTOR), FACTOR ** -0.5, 1.0, (), jnp.float32)
    eigen_values = jnp.clip(jnp.exp(jax.random.uniform(keys[7], (MODULES, FEAT), jnp.float32, math.log(0.05), math.log(5.0))), 0.05, 5.0)
    return dict(query_grads=query_grads, train_grads=train_grads, token_counts=token_counts, query_owner=query_owner, module_map=module_map, out_basis=out_basis, in_basis=in_basis, eigen_values=eigen_values)


damping_value = 0.1


def query_slot(grads, side_out, side_in, values):
    count = grads.shape[0]
    right = jnp.dot(grads.reshape(count * FACTOR, FACTOR), side_in, precision=lax.Precision.HIGHEST)
    right = right.reshape(count, FACTOR, FACTOR)
    both = jnp.einsum("op,koj->kpj", side_out, right, precision=lax.Precision.HIGHEST)
    both = both.reshape(count, FEAT) / (values + damping_value)
    return both.astype(jnp.bfloat16)


def train_slot(grads, side_out, side_in_half):
    count = grads.shape[0]
    right = jnp.dot(grads.reshape(count * FACTOR, FACTOR), side_in_half, preferred_element_type=jnp.float32)
    right = right.reshape(count, FACTOR, FACTOR)
    both = jnp.einsum("op,koj->kpj", side_out, right, precision=lax.Precision.HIGHEST)
    return both.reshape(count, FEAT).astype(jnp.bfloat16)


def reference(query_grads, train_grads, token_counts, query_owner, module_map, out_basis, in_basis, eigen_values):
    side_in = jnp.take(in_basis, module_map, axis=0)
    side_out = jnp.take(out_basis, module_map, axis=0)
    side_in_half = side_in.astype(jnp.bfloat16)
    values = jnp.take(eigen_values, module_map, axis=0)
    precond = jnp.stack([query_slot(query_grads[:, slot], side_out[slot], side_in[slot], values[slot]) for slot in range(MODULES)], axis=1)
    flat_query = precond.reshape(QUERIES, MODULES * FEAT)
    blocks = train_grads.reshape(TRAIN // TRAIN_DEV, TRAIN_DEV, MODULES, FEAT)

    def score_block(block):
        rotated = jnp.stack([train_slot(block[:, slot], side_out[slot], side_in_half[slot]) for slot in range(MODULES)], axis=1)
        rotated = rotated.reshape(TRAIN_DEV, MODULES * FEAT)
        return lax.dot_general(flat_query, rotated, (((1,), (1,)), ((), ())), preferred_element_type=jnp.float32)

    parts = lax.map(score_block, blocks)
    raw = jnp.transpose(parts, (1, 0, 2)).reshape(QUERIES, TRAIN)
    ordered = jnp.zeros((QUERIES, TRAIN), jnp.float32).at[query_owner].set(raw)
    return ordered / token_counts.astype(jnp.float32)[None, :]
```

```python
import jax
import jax.numpy as jnp
from jax import lax
from jax.sharding import PartitionSpec as P

FACTOR = 32
FEAT = 1024
damping_value = 0.1
HI = lax.Precision.HIGHEST


def local(query_grads, train_grads, token_counts, query_owner, module_map, out_basis, in_basis, eigen_values):
    slots = train_grads.shape[1]
    mine_q = query_grads.shape[0]
    first = lax.axis_index("mods") * slots
    module_ids = lax.dynamic_slice_in_dim(module_map, first, slots, 0)
    side_out = jnp.take(out_basis, module_ids, axis=0)
    side_in = jnp.take(in_basis, module_ids, axis=0)
    values = jnp.take(eigen_values, module_ids, axis=0).reshape(slots, FACTOR, FACTOR)
    half = side_in.astype(jnp.bfloat16).astype(jnp.float32)
    grads = query_grads.reshape(mine_q, slots, FACTOR, FACTOR)
    right = jnp.einsum("qsoi,sij->soqj", grads, side_in, precision=HI)
    both = jnp.einsum("sop,soqj->spqj", side_out, right, precision=HI)
    precond = (both / (values + damping_value)[:, :, None, :]).astype(jnp.bfloat16).astype(jnp.float32)
    back = jnp.einsum("sop,spqj->soqj", side_out, precond, precision=HI)
    back = jnp.einsum("soqj,sij->qsoi", back, half, precision=HI)
    back = back.astype(jnp.bfloat16).reshape(mine_q, slots * FEAT)
    full = lax.all_gather(back, "rows", axis=0, tiled=True)
    total = full.shape[0]
    hot = (jnp.arange(total, dtype=jnp.int32)[:, None] == query_owner[None, :]).astype(jnp.bfloat16)
    ordered = jnp.dot(hot, full, preferred_element_type=jnp.float32).astype(jnp.bfloat16)
    raw = lax.dot_general(
        ordered, train_grads.reshape(train_grads.shape[0], slots * FEAT), (((1,), (1,)), ((), ())),
        preferred_element_type=jnp.float32,
    )
    mine = lax.psum_scatter(raw, "mods", scatter_dimension=0, tiled=True)
    return mine / token_counts.astype(jnp.float32)[None, :]


def solution(mesh):
    in_specs = (
        P(("groups", "rows"), "mods", None),
        P(("groups", "rows"), "mods", None),
        P(("groups", "rows")),
        P("groups"),
        P(),
        P(),
        P(),
        P(),
    )
    out_specs = P(("groups", "mods"), "rows")
    return jax.shard_map(local, mesh=mesh, in_specs=in_specs, out_specs=out_specs, check_vma=False)
```

```python
import functools
import jax
import jax.numpy as jnp
from jax import lax
from jax.experimental import pallas as pl
from jax.experimental.pallas import tpu as pltpu
from jax.sharding import PartitionSpec as P

FACTOR = 32
FEAT = 1024
LANES = 128
TILE = 256
damping_value = 0.1
HI = lax.Precision.HIGHEST
MESH = pl.DeviceIdType.MESH


def kernel(
    rows, mods, back_ref, train_ref, owner_ref, counts_ref, out_ref,
    staged, train, full, raw, outgoing, incoming,
    train_sem, far_send, mate_send, gather_recv, sum_send, sum_recv,
):
    slots, mine_q, feat = back_ref.shape
    total_q = full.shape[1]
    train_rows = train.shape[1]
    tiles = train_rows // TILE
    block = out_ref.shape[0]
    columns = feat // LANES
    per_row = columns * slots
    chips = rows // 2
    me = lax.axis_index("rows")
    my_mod = lax.axis_index("mods")
    core = lax.rem(me, 2)
    mate = me + 1 - 2 * core
    fars = [lax.rem(me + 2 * hop, rows) for hop in range(1, chips)]
    others = [lax.rem(my_mod + hop, mods) for hop in range(1, mods)]

    barrier = pltpu.get_barrier_semaphore()
    for row in [mate] + fars:
        pl.semaphore_signal(barrier, inc=1, device_id={"rows": row}, device_id_type=MESH)
    for mod in others:
        pl.semaphore_signal(barrier, inc=1, device_id={"mods": mod}, device_id_type=MESH)

    segment = train_rows // slots
    loads = []
    for part in range(slots):
        span = pl.ds(part * segment * per_row, segment * per_row)
        load = pltpu.make_async_copy(train_ref.at[span], staged.at[span], train_sem.at[part])
        load.start()
        loads.append(load)

    def place(row):
        return pl.ds(pl.multiple_of(row * mine_q, mine_q), mine_q)

    for slot in range(slots):
        full[slot, place(me), :] = back_ref[slot]

    pl.semaphore_wait(barrier, 1 + len(fars) + len(others))

    def gather_copy(slot, owner, to, send):
        return pltpu.make_async_remote_copy(
            src_ref=full.at[slot, place(owner)],
            dst_ref=full.at[slot, place(owner)],
            send_sem=send,
            recv_sem=gather_recv.at[slot, owner],
            device_id={"rows": to},
            device_id_type=MESH,
        )

    sent = []
    for slot in range(slots):
        for hop, far in enumerate(fars):
            copy = gather_copy(slot, me, far, far_send.at[slot, hop])
            copy.start()
            sent.append(copy)
    for slot in range(slots):
        copy = gather_copy(slot, me, mate, mate_send.at[slot, 0])
        copy.start()
        sent.append(copy)

    size = 8 * per_row
    target = lax.broadcasted_iota(jnp.int32, (size, size), 0)
    source = lax.broadcasted_iota(jnp.int32, (size, size), 1)
    wanted = lax.rem(target, 8) * per_row + lax.rem(lax.div(target, 8), columns) * slots + lax.div(target, 8 * columns)
    sorter = (wanted == source).astype(jnp.float32).astype(jnp.bfloat16)

    def sort_segment(part):
        loads[part].wait()

        def step(i, carry):
            base = pl.multiple_of(i * 2 * size, 2 * size)
            first = jnp.dot(sorter, staged[pl.ds(base, size), :], preferred_element_type=jnp.float32)
            second = jnp.dot(sorter, staged[pl.ds(base + size, size), :], preferred_element_type=jnp.float32)
            where = pl.ds(pl.multiple_of(i * 16, 16), 16)
            for slot in range(slots):
                for column in range(columns):
                    at = (slot * columns + column) * 8
                    both = jnp.concatenate([first[at:at + 8], second[at:at + 8]], axis=0)
                    train[slot, where, column * LANES:(column + 1) * LANES] = both.astype(jnp.bfloat16)
            return carry

        steps = segment // 16
        lax.fori_loop(part * steps, (part + 1) * steps, step, 0)

    def forward(slot):
        for hop, far in enumerate(fars):
            gather_copy(slot, far, far, far_send.at[slot, hop]).wait_recv()
            copy = gather_copy(slot, far, mate, mate_send.at[slot, 1 + hop])
            copy.start()
            sent.append(copy)

    ids = lax.broadcasted_iota(jnp.int32, (total_q, total_q), 0)
    hot = (ids == owner_ref[...]).astype(jnp.float32).astype(jnp.bfloat16)

    def ordered(slot):
        gather_copy(slot, mate, mate, mate_send.at[slot, 0]).wait_recv()
        for far in fars:
            near = far + 1 - 2 * core
            gather_copy(slot, near, mate, mate_send.at[slot, 0]).wait_recv()
        return jnp.dot(hot, full[slot], preferred_element_type=jnp.float32).astype(jnp.bfloat16)

    def product(left, slot, tile):
        right = train[slot, tile * TILE:(tile + 1) * TILE, :]
        return lax.dot_general(left, right, (((1,), (1,)), ((), ())), preferred_element_type=jnp.float32)

    def accumulate(slot):
        left = ordered(slot)
        for tile in range(tiles):
            if slot == 0:
                raw[tile] = product(left, slot, tile)
            else:
                raw[tile] += product(left, slot, tile)

    def chunk(mod):
        return pl.ds(pl.multiple_of(mod * block, block), block)

    def sum_copy(tile, hop, to, landing):
        return pltpu.make_async_remote_copy(
            src_ref=outgoing.at[tile, chunk(to)],
            dst_ref=incoming.at[tile, landing],
            send_sem=sum_send.at[tile, hop],
            recv_sem=sum_recv.at[tile, landing],
            device_id={"mods": to},
            device_id_type=MESH,
        )

    half = slots // 2
    for part in range(half):
        sort_segment(part)
        forward(part)
    for part in range(half, slots):
        sort_segment(part)
    for slot in range(half):
        accumulate(slot)
    for slot in range(half, slots - 1):
        forward(slot)
        accumulate(slot)
    forward(slots - 1)
    left = ordered(slots - 1)
    for tile in range(tiles):
        done = raw[tile] + product(left, slots - 1, tile)
        raw[tile] = done
        outgoing[tile] = done.astype(jnp.bfloat16)
        for hop, mod in enumerate(others):
            copy = sum_copy(tile, hop, mod, mods - 2 - hop)
            copy.start()
            sent.append(copy)
    for tile in range(tiles):
        value = raw[tile, chunk(my_mod), :]
        for hop, mod in enumerate(others):
            sum_copy(tile, hop, mod, hop).wait_recv()
            value = value + incoming[tile, hop].astype(jnp.float32)
        where = slice(tile * TILE, (tile + 1) * TILE)
        out_ref[:, where] = value / counts_ref[:, where]
    for copy in sent:
        copy.wait_send()


def score(rows, mods, back, train_grads, owner, counts):
    slots, mine_q, feat = back.shape
    train_rows = train_grads.shape[0]
    columns = feat // LANES
    total_q = rows * mine_q
    tiles = train_rows // TILE
    block = total_q // mods
    staged = train_grads.reshape(train_rows, slots, columns, LANES).transpose(0, 2, 1, 3).reshape(-1, LANES)
    vmem = pl.BlockSpec(memory_space=pltpu.VMEM)
    chips = rows // 2
    return pl.pallas_call(
        functools.partial(kernel, rows, mods),
        out_shape=jax.ShapeDtypeStruct((block, train_rows), jnp.float32),
        in_specs=[vmem, pl.BlockSpec(memory_space=pl.ANY), vmem, vmem],
        out_specs=vmem,
        scratch_shapes=[
            pltpu.VMEM(staged.shape, jnp.bfloat16),
            pltpu.VMEM((slots, train_rows, feat), jnp.bfloat16),
            pltpu.VMEM((slots, total_q, feat), jnp.bfloat16),
            pltpu.VMEM((tiles, total_q, TILE), jnp.float32),
            pltpu.VMEM((tiles, total_q, TILE), jnp.bfloat16),
            pltpu.VMEM((tiles, mods - 1, block, TILE), jnp.bfloat16),
            pltpu.SemaphoreType.DMA((slots,)),
            pltpu.SemaphoreType.DMA((slots, max(chips - 1, 1))),
            pltpu.SemaphoreType.DMA((slots, chips)),
            pltpu.SemaphoreType.DMA((slots, rows)),
            pltpu.SemaphoreType.DMA((tiles, mods - 1)),
            pltpu.SemaphoreType.DMA((tiles, mods - 1)),
        ],
        compiler_params=pltpu.CompilerParams(
            collective_id=0, has_side_effects=True, vmem_limit_bytes=56 * 1024 * 1024
        ),
        name="score",
    )(back, staged, owner, counts)


def local(rows, mods, query_grads, train_grads, token_counts, query_owner, module_map, out_basis, in_basis, eigen_values):
    slots = train_grads.shape[1]
    mine_q = query_grads.shape[0]
    first = lax.axis_index("mods") * slots
    module_ids = lax.dynamic_slice_in_dim(module_map, first, slots, 0)
    side_out = jnp.take(out_basis, module_ids, axis=0)
    side_in = jnp.take(in_basis, module_ids, axis=0)
    values = jnp.take(eigen_values, module_ids, axis=0).reshape(slots, FACTOR, FACTOR)
    half = side_in.astype(jnp.bfloat16).astype(jnp.float32)
    grads = query_grads.reshape(mine_q, slots, FACTOR, FACTOR)
    right = jnp.einsum("qsoi,sij->soqj", grads, side_in, precision=HI)
    both = jnp.einsum("sop,soqj->spqj", side_out, right, precision=HI)
    precond = (both / (values + damping_value)[:, :, None, :]).astype(jnp.bfloat16).astype(jnp.float32)
    back = jnp.einsum("sop,spqj->soqj", side_out, precond, precision=HI)
    back = jnp.einsum("soqj,sij->sqoi", back, half, precision=HI)
    back = back.astype(jnp.bfloat16).reshape(slots, mine_q, FEAT)
    return score(rows, mods, back, train_grads, query_owner[None, :], token_counts.astype(jnp.float32)[None, :])


def solution(mesh):
    in_specs = (
        P(("groups", "rows"), "mods", None),
        P(("groups", "rows"), "mods", None),
        P(("groups", "rows")),
        P("groups"),
        P(),
        P(),
        P(),
        P(),
    )
    out_specs = P(("groups", "mods"), "rows")
    body = functools.partial(local, mesh.shape["rows"], mesh.shape["mods"])
    return jax.shard_map(body, mesh=mesh, in_specs=in_specs, out_specs=out_specs, check_vma=False)
```

```python
import functools
import jax
import jax.numpy as jnp
from jax import lax
from jax.experimental import pallas as pl
from jax.experimental.pallas import tpu as pltpu
from jax.sharding import PartitionSpec as P

FACTOR = 32
FEAT = 1024
LANES = 128
TILE = 256
damping_value = 0.1
MESH = pl.DeviceIdType.MESH


def split(value):
    high = value.astype(jnp.bfloat16)
    return high, (value - high.astype(jnp.float32)).astype(jnp.bfloat16)


def mask(value):
    return value.astype(jnp.float32).astype(jnp.bfloat16)


def rotate(
    slots, my_mod, query_ref, map_ref, out_basis_ref, in_basis_ref, eigen_ref,
    spread, right_ref, precond_ref, back_ref, damped, full, place,
):
    mine_q = right_ref.shape[1]
    columns = FEAT // LANES
    group = LANES // FACTOR
    wide = group * LANES
    modules = [map_ref[my_mod * slots + slot] for slot in range(slots)]
    iota = lambda shape, axis: lax.broadcasted_iota(jnp.int32, shape, axis)
    dot = functools.partial(jnp.dot, preferred_element_type=jnp.float32)

    repeat = mask(iota((FACTOR, wide), 0) == lax.rem(iota((FACTOR, wide), 1), FACTOR))
    lane = iota((LANES, wide), 1)
    same_row = lax.div(iota((LANES, wide), 0), FACTOR) == lax.div(lane, LANES)
    highs, lows = [], []
    for slot in range(slots):
        side_in = in_basis_ref[modules[slot]]
        keep = same_row & (lax.div(lax.rem(lane, LANES), FACTOR) == slot)
        for value, parts in zip(split(jnp.concatenate([side_in] * group, axis=0)), (highs, lows)):
            parts.append(jnp.where(keep, dot(value, repeat), 0.0).astype(jnp.bfloat16))
    block_high = jnp.concatenate(highs, axis=0)
    block_low = jnp.concatenate(lows, axis=0)

    shape = (slots * FACTOR, FACTOR * LANES)
    row, lane = iota(shape, 0), iota(shape, 1)
    pick = mask(
        (lax.rem(row, FACTOR) == lax.div(lane, LANES))
        & (lax.div(row, FACTOR) == lax.div(lax.rem(lane, LANES), FACTOR))
    )
    sides = jnp.concatenate([out_basis_ref[modules[slot]] for slot in range(slots)], axis=0)
    over = lambda left: lax.dot_general(left, pick, (((0,), (0,)), ((), ())), preferred_element_type=jnp.float32)
    high = sides.astype(jnp.bfloat16)
    rest = sides - high.astype(jnp.float32)
    middle, low = split(rest)
    spread_all = over(high) + (over(middle) + over(low))
    for o in range(FACTOR):
        spread[o] = spread_all[:, o * LANES:(o + 1) * LANES]

    shape = (FACTOR, FEAT)
    own = lax.div(iota(shape, 1), FACTOR) == iota(shape, 0)
    fold = mask(lax.rem(iota((FEAT, LANES), 0), FACTOR) == lax.rem(iota((FEAT, LANES), 1), FACTOR))
    slot_of = lax.div(iota((FACTOR, LANES), 1), FACTOR)
    values = jnp.zeros((FACTOR, LANES), jnp.float32)
    for slot in range(slots):
        rows = jnp.where(own, eigen_ref[pl.ds(modules[slot], 1), :], 0.0)
        high = rows.astype(jnp.bfloat16)
        middle, low = split(rows - high.astype(jnp.float32))
        values = jnp.where(slot_of == slot, dot(high, fold) + (dot(middle, fold) + dot(low, fold)), values)
    damped[...] = values + damping_value

    for column in range(columns):
        grads = jnp.concatenate(
            [query_ref[pl.ds(column * slots + slot, mine_q, stride=columns * slots), :] for slot in range(slots)], axis=1
        )
        high, low = split(grads)
        right = dot(high, block_high) + (dot(low, block_high) + dot(high, block_low))
        for o in range(group):
            right_ref[column * group + o] = right[:, o * LANES:(o + 1) * LANES]

    def forth(pair, carry):
        p = pair * 2
        sums = [jnp.zeros((mine_q, LANES), jnp.float32) for _ in range(2)]
        for o in range(FACTOR):
            right = right_ref[o]
            for k in range(2):
                sums[k] = sums[k] + right * spread[o, pl.ds(p + k, 1), :]
        for k in range(2):
            value = sums[k] / damped[pl.ds(p + k, 1), :]
            precond_ref[p + k] = value.astype(jnp.bfloat16).astype(jnp.float32)
        return carry

    lax.fori_loop(0, FACTOR // 2, forth, 0)

    def back(pair, carry):
        o = pair * 2
        sums = [jnp.zeros((mine_q, LANES), jnp.float32) for _ in range(2)]
        for p in range(FACTOR):
            value = precond_ref[p]
            for k in range(2):
                sums[k] = sums[k] + value * spread[o + k, p:p + 1, :]
        for k in range(2):
            back_ref[o + k] = sums[k]
        return carry

    lax.fori_loop(0, FACTOR // 2, back, 0)

    turn = lambda left: lax.dot_general(
        left, block_high, (((1,), (1,)), ((), ())), preferred_element_type=jnp.float32
    )
    for column in range(columns):
        value = jnp.concatenate([back_ref[column * group + o] for o in range(group)], axis=1)
        high, low = split(value)
        result = (turn(high) + turn(low)).astype(jnp.bfloat16)
        for slot in range(slots):
            full[slot, place, column * LANES:(column + 1) * LANES] = result[:, slot * LANES:(slot + 1) * LANES]


def kernel(
    rows, mods, query_ref, train_ref, owner_ref, counts_ref, map_ref, out_basis_ref, in_basis_ref, eigen_ref, out_ref,
    spread, right_ref, precond_ref, back_ref, damped,
    staged, train, full, raw, outgoing, incoming,
    train_sem, far_send, mate_send, gather_recv, sum_send, sum_recv,
):
    slots, train_rows, feat = train.shape
    mine_q = right_ref.shape[1]
    total_q = full.shape[1]
    tiles = train_rows // TILE
    block = out_ref.shape[0]
    columns = feat // LANES
    per_row = columns * slots
    chips = rows // 2
    me = lax.axis_index("rows")
    my_mod = lax.axis_index("mods")
    core = lax.rem(me, 2)
    mate = me + 1 - 2 * core
    fars = [lax.rem(me + 2 * hop, rows) for hop in range(1, chips)]
    others = [lax.rem(my_mod + hop, mods) for hop in range(1, mods)]

    barrier = pltpu.get_barrier_semaphore()
    for row in [mate] + fars:
        pl.semaphore_signal(barrier, inc=1, device_id={"rows": row}, device_id_type=MESH)
    for mod in others:
        pl.semaphore_signal(barrier, inc=1, device_id={"mods": mod}, device_id_type=MESH)

    segment = train_rows // slots
    loads = []
    for part in range(slots):
        span = pl.ds(part * segment * per_row, segment * per_row)
        load = pltpu.make_async_copy(train_ref.at[span], staged.at[span], train_sem.at[part])
        load.start()
        loads.append(load)

    def place(row):
        return pl.ds(pl.multiple_of(row * mine_q, mine_q), mine_q)

    rotate(
        slots, my_mod, query_ref, map_ref, out_basis_ref, in_basis_ref, eigen_ref,
        spread, right_ref, precond_ref, back_ref, damped, full, place(me),
    )

    pl.semaphore_wait(barrier, 1 + len(fars) + len(others))

    def gather_copy(slot, owner, to, send):
        return pltpu.make_async_remote_copy(
            src_ref=full.at[slot, place(owner)],
            dst_ref=full.at[slot, place(owner)],
            send_sem=send,
            recv_sem=gather_recv.at[slot, owner],
            device_id={"rows": to},
            device_id_type=MESH,
        )

    sent = []
    for slot in range(slots):
        for hop, far in enumerate(fars):
            copy = gather_copy(slot, me, far, far_send.at[slot, hop])
            copy.start()
            sent.append(copy)
    for slot in range(slots):
        copy = gather_copy(slot, me, mate, mate_send.at[slot, 0])
        copy.start()
        sent.append(copy)

    size = 8 * per_row
    target = lax.broadcasted_iota(jnp.int32, (size, size), 0)
    source = lax.broadcasted_iota(jnp.int32, (size, size), 1)
    wanted = lax.rem(target, 8) * per_row + lax.rem(lax.div(target, 8), columns) * slots + lax.div(target, 8 * columns)
    sorter = (wanted == source).astype(jnp.float32).astype(jnp.bfloat16)

    def sort_segment(part):
        loads[part].wait()

        def step(i, carry):
            base = pl.multiple_of(i * 2 * size, 2 * size)
            first = jnp.dot(sorter, staged[pl.ds(base, size), :], preferred_element_type=jnp.float32)
            second = jnp.dot(sorter, staged[pl.ds(base + size, size), :], preferred_element_type=jnp.float32)
            where = pl.ds(pl.multiple_of(i * 16, 16), 16)
            for slot in range(slots):
                for column in range(columns):
                    at = (slot * columns + column) * 8
                    both = jnp.concatenate([first[at:at + 8], second[at:at + 8]], axis=0)
                    train[slot, where, column * LANES:(column + 1) * LANES] = both.astype(jnp.bfloat16)
            return carry

        steps = segment // 16
        lax.fori_loop(part * steps, (part + 1) * steps, step, 0)

    def forward(slot):
        for hop, far in enumerate(fars):
            gather_copy(slot, far, far, far_send.at[slot, hop]).wait_recv()
            copy = gather_copy(slot, far, mate, mate_send.at[slot, 1 + hop])
            copy.start()
            sent.append(copy)

    ids = lax.broadcasted_iota(jnp.int32, (total_q, total_q), 0)
    hot = (ids == owner_ref[...]).astype(jnp.float32).astype(jnp.bfloat16)

    def ordered(slot):
        gather_copy(slot, mate, mate, mate_send.at[slot, 0]).wait_recv()
        for far in fars:
            near = far + 1 - 2 * core
            gather_copy(slot, near, mate, mate_send.at[slot, 0]).wait_recv()
        return jnp.dot(hot, full[slot], preferred_element_type=jnp.float32).astype(jnp.bfloat16)

    def product(left, slot, tile):
        right = train[slot, tile * TILE:(tile + 1) * TILE, :]
        return lax.dot_general(left, right, (((1,), (1,)), ((), ())), preferred_element_type=jnp.float32)

    def accumulate(slot):
        left = ordered(slot)
        for tile in range(tiles):
            if slot == 0:
                raw[tile] = product(left, slot, tile)
            else:
                raw[tile] += product(left, slot, tile)

    def chunk(mod):
        return pl.ds(pl.multiple_of(mod * block, block), block)

    def sum_copy(tile, hop, to, landing):
        return pltpu.make_async_remote_copy(
            src_ref=outgoing.at[tile, chunk(to)],
            dst_ref=incoming.at[tile, landing],
            send_sem=sum_send.at[tile, hop],
            recv_sem=sum_recv.at[tile, landing],
            device_id={"mods": to},
            device_id_type=MESH,
        )

    half = slots // 2
    for part in range(half):
        sort_segment(part)
        forward(part)
    for part in range(half, slots):
        sort_segment(part)
    for slot in range(half):
        accumulate(slot)
    for slot in range(half, slots - 1):
        forward(slot)
        accumulate(slot)
    forward(slots - 1)
    left = ordered(slots - 1)
    for tile in range(tiles):
        done = raw[tile] + product(left, slots - 1, tile)
        raw[tile] = done
        outgoing[tile] = done.astype(jnp.bfloat16)
        for hop, mod in enumerate(others):
            copy = sum_copy(tile, hop, mod, mods - 2 - hop)
            copy.start()
            sent.append(copy)
    for tile in range(tiles):
        value = raw[tile, chunk(my_mod), :]
        for hop, mod in enumerate(others):
            sum_copy(tile, hop, mod, hop).wait_recv()
            value = value + incoming[tile, hop].astype(jnp.float32)
        where = slice(tile * TILE, (tile + 1) * TILE)
        out_ref[:, where] = value / counts_ref[:, where].astype(jnp.float32)
    for copy in sent:
        copy.wait_send()


def local(rows, mods, query_grads, train_grads, token_counts, query_owner, module_map, out_basis, in_basis, eigen_values):
    mine_q = query_grads.shape[0]
    train_rows, slots, feat = train_grads.shape
    columns = feat // LANES
    total_q = rows * mine_q
    tiles = train_rows // TILE
    block = total_q // mods
    staged = train_grads.reshape(train_rows, slots, columns, LANES).transpose(0, 2, 1, 3).reshape(-1, LANES)
    queries = query_grads.reshape(mine_q, slots, columns, LANES).transpose(0, 2, 1, 3).reshape(-1, LANES)
    owner = query_owner[None, :]
    counts = token_counts[None, :]
    vmem = pl.BlockSpec(memory_space=pltpu.VMEM)
    chips = rows // 2
    return pl.pallas_call(
        functools.partial(kernel, rows, mods),
        out_shape=jax.ShapeDtypeStruct((block, train_rows), jnp.float32),
        in_specs=[vmem, pl.BlockSpec(memory_space=pl.ANY), vmem, vmem, pl.BlockSpec(memory_space=pltpu.SMEM), vmem, vmem, vmem],
        out_specs=vmem,
        scratch_shapes=[
            pltpu.VMEM((FACTOR, FACTOR, LANES), jnp.float32),
            pltpu.VMEM((FACTOR, mine_q, LANES), jnp.float32),
            pltpu.VMEM((FACTOR, mine_q, LANES), jnp.float32),
            pltpu.VMEM((FACTOR, mine_q, LANES), jnp.float32),
            pltpu.VMEM((FACTOR, LANES), jnp.float32),
            pltpu.VMEM(staged.shape, jnp.bfloat16),
            pltpu.VMEM((slots, train_rows, feat), jnp.bfloat16),
            pltpu.VMEM((slots, total_q, feat), jnp.bfloat16),
            pltpu.VMEM((tiles, total_q, TILE), jnp.float32),
            pltpu.VMEM((tiles, total_q, TILE), jnp.bfloat16),
            pltpu.VMEM((tiles, mods - 1, block, TILE), jnp.bfloat16),
            pltpu.SemaphoreType.DMA((slots,)),
            pltpu.SemaphoreType.DMA((slots, max(chips - 1, 1))),
            pltpu.SemaphoreType.DMA((slots, chips)),
            pltpu.SemaphoreType.DMA((slots, rows)),
            pltpu.SemaphoreType.DMA((tiles, mods - 1)),
            pltpu.SemaphoreType.DMA((tiles, mods - 1)),
        ],
        compiler_params=pltpu.CompilerParams(
            collective_id=0, has_side_effects=True, vmem_limit_bytes=56 * 1024 * 1024
        ),
        name="score",
    )(queries, staged, owner, counts, module_map, out_basis, in_basis, eigen_values)


def solution(mesh):
    in_specs = (
        P(("groups", "rows"), "mods", None),
        P(("groups", "rows"), "mods", None),
        P(("groups", "rows")),
        P("groups"),
        P(),
        P(),
        P(),
        P(),
    )
    out_specs = P(("groups", "mods"), "rows")
    body = functools.partial(local, mesh.shape["rows"], mesh.shape["mods"])
    return jax.shard_map(body, mesh=mesh, in_specs=in_specs, out_specs=out_specs, check_vma=False)
```

```python
import functools
import jax
import jax.numpy as jnp
from jax import lax
from jax.experimental import pallas as pl
from jax.experimental.pallas import tpu as pltpu
from jax.sharding import PartitionSpec as P

FACTOR = 32
FEAT = 1024
LANES = 128
FACTOR_BITS = 5
LANE_BITS = 7
HALVES = 2
TILE = 256
damping_value = 0.1
MESH = pl.DeviceIdType.MESH


def split(value):
    high = value.astype(jnp.bfloat16)
    return high, (value - high.astype(jnp.float32)).astype(jnp.bfloat16)


def mask(value):
    return value.astype(jnp.float32).astype(jnp.bfloat16)


def rotate(
    slots, my_mod, query_ref, map_ref, out_basis_ref, in_basis_ref, eigen_ref,
    spread, right_ref, precond_ref, back_ref, damped, full, place,
):
    mine_q = right_ref.shape[1] * HALVES
    columns = FEAT // LANES
    group = LANES // FACTOR
    wide = group * LANES
    modules = [map_ref[my_mod * slots + slot] for slot in range(slots)]
    iota = lambda shape, axis: lax.broadcasted_iota(jnp.int32, shape, axis)
    dot = functools.partial(jnp.dot, preferred_element_type=jnp.float32)

    repeat = mask(iota((FACTOR, wide), 0) == (iota((FACTOR, wide), 1) & (FACTOR - 1)))
    lane = iota((LANES, wide), 1)
    same_row = (iota((LANES, wide), 0) >> FACTOR_BITS) == (lane >> LANE_BITS)
    highs, lows = [], []
    for slot in range(slots):
        side_in = in_basis_ref[modules[slot]]
        keep = same_row & (((lane & (LANES - 1)) >> FACTOR_BITS) == slot)
        for value, parts in zip(split(jnp.concatenate([side_in] * group, axis=0)), (highs, lows)):
            parts.append(jnp.where(keep, dot(value, repeat), 0.0).astype(jnp.bfloat16))
    block_high = jnp.concatenate(highs, axis=0)
    block_low = jnp.concatenate(lows, axis=0)

    shape = (slots * FACTOR, FACTOR * LANES)
    row, lane = iota(shape, 0), iota(shape, 1)
    pick = mask(
        ((row & (FACTOR - 1)) == (lane >> LANE_BITS))
        & ((row >> FACTOR_BITS) == ((lane & (LANES - 1)) >> FACTOR_BITS))
    )
    sides = jnp.concatenate([out_basis_ref[modules[slot]] for slot in range(slots)], axis=0)
    over = lambda left: lax.dot_general(left, pick, (((0,), (0,)), ((), ())), preferred_element_type=jnp.float32)
    high = sides.astype(jnp.bfloat16)
    rest = sides - high.astype(jnp.float32)
    middle, low = split(rest)
    spread_all = over(high) + (over(middle) + over(low))
    for o in range(FACTOR):
        spread[o] = spread_all[:, o * LANES:(o + 1) * LANES]

    shape = (FACTOR, FEAT)
    own = (iota(shape, 1) >> FACTOR_BITS) == iota(shape, 0)
    fold = mask((iota((FEAT, LANES), 0) & (FACTOR - 1)) == (iota((FEAT, LANES), 1) & (FACTOR - 1)))
    slot_of = iota((FACTOR, LANES), 1) >> FACTOR_BITS
    values = jnp.zeros((FACTOR, LANES), jnp.float32)
    for slot in range(slots):
        rows = jnp.where(own, eigen_ref[pl.ds(modules[slot], 1), :], 0.0)
        high = rows.astype(jnp.bfloat16)
        middle, low = split(rows - high.astype(jnp.float32))
        values = jnp.where(slot_of == slot, dot(high, fold) + (dot(middle, fold) + dot(low, fold)), values)
    damped[...] = values + damping_value

    turn = lambda left: lax.dot_general(
        left, block_high, (((1,), (1,)), ((), ())), preferred_element_type=jnp.float32
    )
    count = mine_q // HALVES
    together = 4

    def run(half):
        start = half * count
        for column in range(columns):
            grads = jnp.concatenate(
                [
                    query_ref[pl.ds((start * columns + column) * slots + slot, count, stride=columns * slots), :]
                    for slot in range(slots)
                ],
                axis=1,
            )
            high, low = split(grads)
            right = dot(high, block_high) + (dot(low, block_high) + dot(high, block_low))
            for o in range(group):
                right_ref[column * group + o] = right[:, o * LANES:(o + 1) * LANES]

        def forth(step, carry):
            p = step * together
            sums = [jnp.zeros((count, LANES), jnp.float32) for _ in range(together)]
            for o in range(FACTOR):
                right = right_ref[o]
                for k in range(together):
                    sums[k] = sums[k] + right * spread[o, pl.ds(p + k, 1), :]
            for k in range(together):
                value = sums[k] / damped[pl.ds(p + k, 1), :]
                precond_ref[p + k] = value.astype(jnp.bfloat16).astype(jnp.float32)
            return carry

        lax.fori_loop(0, FACTOR // together, forth, 0)

        def back(step, carry):
            o = step * together
            sums = [jnp.zeros((count, LANES), jnp.float32) for _ in range(together)]
            for p in range(FACTOR):
                value = precond_ref[p]
                for k in range(together):
                    sums[k] = sums[k] + value * spread[o + k, p:p + 1, :]
            for k in range(together):
                back_ref[o + k] = sums[k]
            return carry

        lax.fori_loop(0, FACTOR // together, back, 0)

        for column in range(columns):
            value = jnp.concatenate([back_ref[column * group + o] for o in range(group)], axis=1)
            high, low = split(value)
            result = (turn(high) + turn(low)).astype(jnp.bfloat16)
            for slot in range(slots):
                full[slot, place(half), column * LANES:(column + 1) * LANES] = result[:, slot * LANES:(slot + 1) * LANES]

    return run


def kernel(
    rows, mods, query_ref, train_ref, owner_ref, counts_ref, map_ref, out_basis_ref, in_basis_ref, eigen_ref, out_ref,
    spread, right_ref, precond_ref, back_ref, damped,
    staged, train, full, raw, outgoing, incoming,
    train_sem, far_send, mate_send, gather_recv, sum_send, sum_recv,
):
    slots, train_rows, feat = train.shape
    mine_q = right_ref.shape[1] * HALVES
    total_q = full.shape[1]
    tiles = train_rows // TILE
    block = out_ref.shape[0]
    columns = feat // LANES
    per_row = columns * slots
    chips = rows // 2
    me = lax.axis_index("rows")
    my_mod = lax.axis_index("mods")
    core = lax.rem(me, 2)
    mate = me + 1 - 2 * core
    fars = [lax.rem(me + 2 * hop, rows) for hop in range(1, chips)]
    others = [lax.rem(my_mod + hop, mods) for hop in range(1, mods)]

    barrier = pltpu.get_barrier_semaphore()
    for row in [mate] + fars:
        pl.semaphore_signal(barrier, inc=1, device_id={"rows": row}, device_id_type=MESH)
    for mod in others:
        pl.semaphore_signal(barrier, inc=1, device_id={"mods": mod}, device_id_type=MESH)

    segment = train_rows // slots
    loads = []
    for part in range(slots):
        span = pl.ds(part * segment * per_row, segment * per_row)
        load = pltpu.make_async_copy(train_ref.at[span], staged.at[span], train_sem.at[part])
        load.start()
        loads.append(load)

    count = mine_q // HALVES

    def place(row, half):
        return pl.ds(pl.multiple_of(row * mine_q + half * count, count), count)

    def gather_copy(half, slot, owner, to, send):
        return pltpu.make_async_remote_copy(
            src_ref=full.at[slot, place(owner, half)],
            dst_ref=full.at[slot, place(owner, half)],
            send_sem=send,
            recv_sem=gather_recv.at[half, slot, owner],
            device_id={"rows": to},
            device_id_type=MESH,
        )

    run = rotate(
        slots, my_mod, query_ref, map_ref, out_basis_ref, in_basis_ref, eigen_ref,
        spread, right_ref, precond_ref, back_ref, damped, full, functools.partial(place, me),
    )
    sent = []
    for half in range(HALVES):
        run(half)
        if half == 0:
            pl.semaphore_wait(barrier, 1 + len(fars) + len(others))
        for slot in range(slots):
            for hop, far in enumerate(fars):
                copy = gather_copy(half, slot, me, far, far_send.at[half, slot, hop])
                copy.start()
                sent.append(copy)
            copy = gather_copy(half, slot, me, mate, mate_send.at[half, slot, 0])
            copy.start()
            sent.append(copy)

    size = 8 * per_row
    target = lax.broadcasted_iota(jnp.int32, (size, size), 0)
    source = lax.broadcasted_iota(jnp.int32, (size, size), 1)
    bits = columns.bit_length() - 1
    wanted = (target & 7) * per_row + ((target >> 3) & (columns - 1)) * slots + (target >> (3 + bits))
    sorter = (wanted == source).astype(jnp.float32).astype(jnp.bfloat16)

    def sort_segment(part):
        loads[part].wait()

        def step(i, carry):
            base = pl.multiple_of(i * 2 * size, 2 * size)
            pair = jnp.concatenate([staged[pl.ds(base, size), :], staged[pl.ds(base + size, size), :]], axis=1)
            done = jnp.dot(sorter, pair, preferred_element_type=jnp.float32)
            where = pl.ds(pl.multiple_of(i * 16, 16), 16)
            for slot in range(slots):
                for column in range(columns):
                    at = (slot * columns + column) * 8
                    both = jnp.concatenate([done[at:at + 8, :LANES], done[at:at + 8, LANES:]], axis=0)
                    train[slot, where, column * LANES:(column + 1) * LANES] = both.astype(jnp.bfloat16)
            return carry

        steps = segment // 16
        lax.fori_loop(0, steps // 4, lambda i, carry: [step(part * steps + i * 4 + k, carry) for k in range(4)][-1], 0)

    def forward(half, slot):
        for hop, far in enumerate(fars):
            gather_copy(half, slot, far, far, far_send.at[half, slot, hop]).wait_recv()
            copy = gather_copy(half, slot, far, mate, mate_send.at[half, slot, 1 + hop])
            copy.start()
            sent.append(copy)

    ids = lax.broadcasted_iota(jnp.int32, (total_q, total_q), 0)
    hot = (ids == owner_ref[...]).astype(jnp.float32).astype(jnp.bfloat16)
    own_ids = lax.broadcasted_iota(jnp.int32, (block, total_q), 0) + my_mod * block
    own_hot = (own_ids == owner_ref[...]).astype(jnp.float32).astype(jnp.bfloat16)

    def against(left, right):
        return lax.dot_general(left, right, (((1,), (1,)), ((), ())), preferred_element_type=jnp.float32)

    def accumulate(slot):
        for half in range(HALVES):
            for owner in [mate] + [far + 1 - 2 * core for far in fars]:
                gather_copy(half, slot, owner, mate, mate_send.at[half, slot, 0]).wait_recv()
        for part in range(raw.shape[0]):
            some = against(train[slot], full[slot, part * TILE:(part + 1) * TILE, :])
            raw[part] = some if slot == 0 else raw[part] + some

    def chunk(mod):
        return pl.ds(pl.multiple_of(mod * block, block), block)

    def sum_copy(tile, hop, to, landing):
        return pltpu.make_async_remote_copy(
            src_ref=outgoing.at[tile, chunk(to)],
            dst_ref=incoming.at[tile, landing],
            send_sem=sum_send.at[tile, hop],
            recv_sem=sum_recv.at[tile, landing],
            device_id={"mods": to},
            device_id_type=MESH,
        )

    for part in range(slots):
        sort_segment(part)
        forward(0, part)
    for slot in range(slots):
        forward(1, slot)
        if slot > 0:
            accumulate(slot - 1)
    accumulate(slots - 1)

    for tile in range(tiles):
        where = slice(tile * TILE, (tile + 1) * TILE)
        ordered = own = 0.0
        for part in range(raw.shape[0]):
            columns_of = slice(part * TILE, (part + 1) * TILE)
            high, low = split(raw[part, where, :])
            ordered = ordered + against(hot[:, columns_of], high)
            own = own + (against(own_hot[:, columns_of], high) + against(own_hot[:, columns_of], low))
        outgoing[tile] = ordered.astype(jnp.bfloat16)
        out_ref[:, where] = own
        for hop, mod in enumerate(others):
            copy = sum_copy(tile, hop, mod, mods - 2 - hop)
            copy.start()
            sent.append(copy)
    for tile in range(tiles):
        where = slice(tile * TILE, (tile + 1) * TILE)
        value = out_ref[:, where]
        for hop, mod in enumerate(others):
            sum_copy(tile, hop, mod, hop).wait_recv()
            value = value + incoming[tile, hop].astype(jnp.float32)
        out_ref[:, where] = value / counts_ref[:, where].astype(jnp.float32)
    for copy in sent:
        copy.wait_send()


def local(rows, mods, query_grads, train_grads, token_counts, query_owner, module_map, out_basis, in_basis, eigen_values):
    mine_q = query_grads.shape[0]
    train_rows, slots, feat = train_grads.shape
    columns = feat // LANES
    total_q = rows * mine_q
    tiles = train_rows // TILE
    block = total_q // mods
    staged = train_grads.reshape(train_rows, slots, columns, LANES).transpose(0, 2, 1, 3).reshape(-1, LANES)
    queries = query_grads.reshape(mine_q, slots, columns, LANES).transpose(0, 2, 1, 3).reshape(-1, LANES)
    owner = query_owner[None, :]
    counts = token_counts[None, :]
    vmem = pl.BlockSpec(memory_space=pltpu.VMEM)
    chips = rows // 2
    return pl.pallas_call(
        functools.partial(kernel, rows, mods),
        out_shape=jax.ShapeDtypeStruct((block, train_rows), jnp.float32),
        in_specs=[vmem, pl.BlockSpec(memory_space=pl.ANY), vmem, vmem, pl.BlockSpec(memory_space=pltpu.SMEM), vmem, vmem, vmem],
        out_specs=vmem,
        scratch_shapes=[
            pltpu.VMEM((FACTOR, FACTOR, LANES), jnp.float32),
            pltpu.VMEM((FACTOR, mine_q // HALVES, LANES), jnp.float32),
            pltpu.VMEM((FACTOR, mine_q // HALVES, LANES), jnp.float32),
            pltpu.VMEM((FACTOR, mine_q // HALVES, LANES), jnp.float32),
            pltpu.VMEM((FACTOR, LANES), jnp.float32),
            pltpu.VMEM(staged.shape, jnp.bfloat16),
            pltpu.VMEM((slots, train_rows, feat), jnp.bfloat16),
            pltpu.VMEM((slots, total_q, feat), jnp.bfloat16),
            pltpu.VMEM((total_q // TILE, train_rows, TILE), jnp.float32),
            pltpu.VMEM((tiles, total_q, TILE), jnp.bfloat16),
            pltpu.VMEM((tiles, mods - 1, block, TILE), jnp.bfloat16),
            pltpu.SemaphoreType.DMA((slots,)),
            pltpu.SemaphoreType.DMA((HALVES, slots, max(chips - 1, 1))),
            pltpu.SemaphoreType.DMA((HALVES, slots, chips)),
            pltpu.SemaphoreType.DMA((HALVES, slots, rows)),
            pltpu.SemaphoreType.DMA((tiles, mods - 1)),
            pltpu.SemaphoreType.DMA((tiles, mods - 1)),
        ],
        compiler_params=pltpu.CompilerParams(
            collective_id=0, has_side_effects=True, vmem_limit_bytes=56 * 1024 * 1024
        ),
        name="score",
    )(queries, staged, owner, counts, module_map, out_basis, in_basis, eigen_values)


def solution(mesh):
    in_specs = (
        P(("groups", "rows"), "mods", None),
        P(("groups", "rows"), "mods", None),
        P(("groups", "rows")),
        P("groups"),
        P(),
        P(),
        P(),
        P(),
    )
    out_specs = P(("groups", "mods"), "rows")
    body = functools.partial(local, mesh.shape["rows"], mesh.shape["mods"])
    return jax.shard_map(body, mesh=mesh, in_specs=in_specs, out_specs=out_specs, check_vma=False)
```

```python
import functools
import jax
import jax.numpy as jnp
from jax import lax
from jax.experimental import pallas as pl
from jax.experimental.pallas import tpu as pltpu
from jax.sharding import PartitionSpec as P

FACTOR = 32
FEAT = 1024
LANES = 128
FACTOR_BITS = 5
LANE_BITS = 7
HALVES = 2
TILE = 256
damping_value = 0.1
MESH = pl.DeviceIdType.MESH


def split(value):
    high = value.astype(jnp.bfloat16)
    return high, (value - high.astype(jnp.float32)).astype(jnp.bfloat16)


def mask(value):
    return value.astype(jnp.float32).astype(jnp.bfloat16)


def rotate(
    slots, my_mod, query_ref, map_ref, out_basis_ref, in_basis_ref, eigen_ref,
    spread, right_ref, precond_ref, back_ref, damped, full, place,
):
    mine_q = right_ref.shape[1] * HALVES
    columns = FEAT // LANES
    group = LANES // FACTOR
    wide = group * LANES
    modules = [map_ref[my_mod * slots + slot] for slot in range(slots)]
    iota = lambda shape, axis: lax.broadcasted_iota(jnp.int32, shape, axis)
    dot = functools.partial(jnp.dot, preferred_element_type=jnp.float32)

    repeat = mask(iota((FACTOR, wide), 0) == (iota((FACTOR, wide), 1) & (FACTOR - 1)))
    lane = iota((LANES, wide), 1)
    same_row = (iota((LANES, wide), 0) >> FACTOR_BITS) == (lane >> LANE_BITS)
    highs, lows = [], []
    for slot in range(slots):
        side_in = in_basis_ref[modules[slot]]
        keep = same_row & (((lane & (LANES - 1)) >> FACTOR_BITS) == slot)
        for value, parts in zip(split(jnp.concatenate([side_in] * group, axis=0)), (highs, lows)):
            parts.append(jnp.where(keep, dot(value, repeat), 0.0).astype(jnp.bfloat16))
    block_high = jnp.concatenate(highs, axis=0)
    block_low = jnp.concatenate(lows, axis=0)

    shape = (slots * FACTOR, FACTOR * LANES)
    row, lane = iota(shape, 0), iota(shape, 1)
    pick = mask(
        ((row & (FACTOR - 1)) == (lane >> LANE_BITS))
        & ((row >> FACTOR_BITS) == ((lane & (LANES - 1)) >> FACTOR_BITS))
    )
    sides = jnp.concatenate([out_basis_ref[modules[slot]] for slot in range(slots)], axis=0)
    over = lambda left: lax.dot_general(left, pick, (((0,), (0,)), ((), ())), preferred_element_type=jnp.float32)
    high = sides.astype(jnp.bfloat16)
    rest = sides - high.astype(jnp.float32)
    middle, low = split(rest)
    spread_all = over(high) + (over(middle) + over(low))
    for o in range(FACTOR):
        spread[o] = spread_all[:, o * LANES:(o + 1) * LANES]

    shape = (FACTOR, FEAT)
    own = (iota(shape, 1) >> FACTOR_BITS) == iota(shape, 0)
    fold = mask((iota((FEAT, LANES), 0) & (FACTOR - 1)) == (iota((FEAT, LANES), 1) & (FACTOR - 1)))
    slot_of = iota((FACTOR, LANES), 1) >> FACTOR_BITS
    values = jnp.zeros((FACTOR, LANES), jnp.float32)
    for slot in range(slots):
        rows = jnp.where(own, eigen_ref[pl.ds(modules[slot], 1), :], 0.0)
        high = rows.astype(jnp.bfloat16)
        middle, low = split(rows - high.astype(jnp.float32))
        values = jnp.where(slot_of == slot, dot(high, fold) + (dot(middle, fold) + dot(low, fold)), values)
    damped[...] = values + damping_value

    turn = lambda left: lax.dot_general(
        left, block_high, (((1,), (1,)), ((), ())), preferred_element_type=jnp.float32
    )
    count = mine_q // HALVES
    together = 4

    def run(half):
        start = half * count
        grads = jnp.concatenate(
            [
                jnp.concatenate(
                    [
                        query_ref[pl.ds((start * columns + column) * slots + slot, count, stride=columns * slots), :]
                        for slot in range(slots)
                    ],
                    axis=1,
                )
                for column in range(columns)
            ],
            axis=0,
        )
        high, low = split(grads)
        size = columns * count
        both = dot(jnp.concatenate([high, low], axis=0), block_high)
        right = both[:size] + (both[size:] + dot(high, block_low))
        for column in range(columns):
            for o in range(group):
                right_ref[column * group + o] = right[column * count:(column + 1) * count, o * LANES:(o + 1) * LANES]

        def forth(step, carry):
            p = step * together
            sums = [jnp.zeros((count, LANES), jnp.float32) for _ in range(together)]
            for o in range(FACTOR):
                right = right_ref[o]
                for k in range(together):
                    sums[k] = sums[k] + right * spread[o, pl.ds(p + k, 1), :]
            for k in range(together):
                value = sums[k] / damped[pl.ds(p + k, 1), :]
                precond_ref[p + k] = value.astype(jnp.bfloat16).astype(jnp.float32)
            return carry

        lax.fori_loop(0, FACTOR // together, forth, 0)

        def back(step, carry):
            o = step * together
            sums = [jnp.zeros((count, LANES), jnp.float32) for _ in range(together)]
            for p in range(FACTOR):
                value = precond_ref[p]
                for k in range(together):
                    sums[k] = sums[k] + value * spread[o + k, p:p + 1, :]
            for k in range(together):
                back_ref[o + k] = sums[k]
            return carry

        lax.fori_loop(0, FACTOR // together, back, 0)

        value = jnp.concatenate(
            [
                jnp.concatenate([back_ref[column * group + o] for o in range(group)], axis=1)
                for column in range(columns)
            ],
            axis=0,
        )
        both = turn(jnp.concatenate(split(value), axis=0))
        result = (both[:size] + both[size:]).astype(jnp.bfloat16)
        for column in range(columns):
            for slot in range(slots):
                full[slot, place(half), column * LANES:(column + 1) * LANES] = result[
                    column * count:(column + 1) * count, slot * LANES:(slot + 1) * LANES
                ]

    return run


def kernel(
    rows, mods, query_ref, train_ref, owner_ref, counts_ref, map_ref, out_basis_ref, in_basis_ref, eigen_ref, out_ref,
    spread, right_ref, precond_ref, back_ref, damped,
    staged, train, full, raw, outgoing, incoming,
    train_sem, far_send, mate_send, gather_recv, sum_send, sum_recv,
):
    slots, train_rows, feat = train.shape
    mine_q = right_ref.shape[1] * HALVES
    total_q = full.shape[1]
    tiles = train_rows // TILE
    block = out_ref.shape[0]
    columns = feat // LANES
    per_row = columns * slots
    chips = rows // 2
    me = lax.axis_index("rows")
    my_mod = lax.axis_index("mods")
    core = lax.rem(me, 2)
    mate = me + 1 - 2 * core
    fars = [lax.rem(me + 2 * hop, rows) for hop in range(1, chips)]
    others = [lax.rem(my_mod + hop, mods) for hop in range(1, mods)]

    barrier = pltpu.get_barrier_semaphore()
    for row in [mate] + fars:
        pl.semaphore_signal(barrier, inc=1, device_id={"rows": row}, device_id_type=MESH)
    for mod in others:
        pl.semaphore_signal(barrier, inc=1, device_id={"mods": mod}, device_id_type=MESH)

    segment = train_rows // slots
    loads = []
    for part in range(slots):
        span = pl.ds(part * segment * per_row, segment * per_row)
        load = pltpu.make_async_copy(train_ref.at[span], staged.at[span], train_sem.at[part])
        load.start()
        loads.append(load)

    count = mine_q // HALVES

    def place(row, half):
        return pl.ds(pl.multiple_of(row * mine_q + half * count, count), count)

    def gather_copy(half, slot, owner, to, send):
        return pltpu.make_async_remote_copy(
            src_ref=full.at[slot, place(owner, half)],
            dst_ref=full.at[slot, place(owner, half)],
            send_sem=send,
            recv_sem=gather_recv.at[half, slot, owner],
            device_id={"rows": to},
            device_id_type=MESH,
        )

    run = rotate(
        slots, my_mod, query_ref, map_ref, out_basis_ref, in_basis_ref, eigen_ref,
        spread, right_ref, precond_ref, back_ref, damped, full, functools.partial(place, me),
    )
    sent = []
    for half in range(HALVES):
        run(half)
        if half == 0:
            pl.semaphore_wait(barrier, 1 + len(fars) + len(others))
        for slot in range(slots):
            for hop, far in enumerate(fars):
                copy = gather_copy(half, slot, me, far, far_send.at[half, slot, hop])
                copy.start()
                sent.append(copy)
            copy = gather_copy(half, slot, me, mate, mate_send.at[half, slot, 0])
            copy.start()
            sent.append(copy)

    size = 8 * per_row
    target = lax.broadcasted_iota(jnp.int32, (size, size), 0)
    source = lax.broadcasted_iota(jnp.int32, (size, size), 1)
    bits = columns.bit_length() - 1
    wanted = (target & 7) * per_row + ((target >> 3) & (columns - 1)) * slots + (target >> (3 + bits))
    sorter = (wanted == source).astype(jnp.float32).astype(jnp.bfloat16)

    def sort_segment(part):
        loads[part].wait()

        def step(i, carry):
            base = pl.multiple_of(i * 2 * size, 2 * size)
            pair = jnp.concatenate([staged[pl.ds(base, size), :], staged[pl.ds(base + size, size), :]], axis=1)
            done = jnp.dot(sorter, pair, preferred_element_type=jnp.float32)
            where = pl.ds(pl.multiple_of(i * 16, 16), 16)
            for slot in range(slots):
                for column in range(columns):
                    at = (slot * columns + column) * 8
                    both = jnp.concatenate([done[at:at + 8, :LANES], done[at:at + 8, LANES:]], axis=0)
                    train[slot, where, column * LANES:(column + 1) * LANES] = both.astype(jnp.bfloat16)
            return carry

        steps = segment // 16
        lax.fori_loop(0, steps // 4, lambda i, carry: [step(part * steps + i * 4 + k, carry) for k in range(4)][-1], 0)

    def forward(half, slot):
        for hop, far in enumerate(fars):
            gather_copy(half, slot, far, far, far_send.at[half, slot, hop]).wait_recv()
            copy = gather_copy(half, slot, far, mate, mate_send.at[half, slot, 1 + hop])
            copy.start()
            sent.append(copy)

    ids = lax.broadcasted_iota(jnp.int32, (total_q, total_q), 0)
    hot = (ids == owner_ref[...]).astype(jnp.float32).astype(jnp.bfloat16)
    own_ids = lax.broadcasted_iota(jnp.int32, (block, total_q), 0) + my_mod * block
    own_hot = (own_ids == owner_ref[...]).astype(jnp.float32).astype(jnp.bfloat16)

    def against(left, right):
        return lax.dot_general(left, right, (((1,), (1,)), ((), ())), preferred_element_type=jnp.float32)

    def accumulate(slot):
        for half in range(HALVES):
            for owner in [mate] + [far + 1 - 2 * core for far in fars]:
                gather_copy(half, slot, owner, mate, mate_send.at[half, slot, 0]).wait_recv()
        for part in range(raw.shape[0]):
            some = against(train[slot], full[slot, part * TILE:(part + 1) * TILE, :])
            raw[part] = some if slot == 0 else raw[part] + some

    def chunk(mod):
        return pl.ds(pl.multiple_of(mod * block, block), block)

    def sum_copy(tile, hop, to, landing):
        return pltpu.make_async_remote_copy(
            src_ref=outgoing.at[tile, chunk(to)],
            dst_ref=incoming.at[tile, landing],
            send_sem=sum_send.at[tile, hop],
            recv_sem=sum_recv.at[tile, landing],
            device_id={"mods": to},
            device_id_type=MESH,
        )

    for part in range(slots):
        sort_segment(part)
        forward(0, part)
    for slot in range(slots):
        forward(1, slot)
        if slot > 0:
            accumulate(slot - 1)
    accumulate(slots - 1)

    for tile in range(tiles):
        where = slice(tile * TILE, (tile + 1) * TILE)
        ordered = own = 0.0
        for part in range(raw.shape[0]):
            columns_of = slice(part * TILE, (part + 1) * TILE)
            high, low = split(raw[part, where, :])
            ordered = ordered + against(hot[:, columns_of], high)
            own = own + (against(own_hot[:, columns_of], high) + against(own_hot[:, columns_of], low))
        outgoing[tile] = ordered.astype(jnp.bfloat16)
        out_ref[:, where] = own
        for hop, mod in enumerate(others):
            copy = sum_copy(tile, hop, mod, mods - 2 - hop)
            copy.start()
            sent.append(copy)
    for tile in range(tiles):
        where = slice(tile * TILE, (tile + 1) * TILE)
        value = out_ref[:, where]
        for hop, mod in enumerate(others):
            sum_copy(tile, hop, mod, hop).wait_recv()
            value = value + incoming[tile, hop].astype(jnp.float32)
        out_ref[:, where] = value / counts_ref[:, where].astype(jnp.float32)
    for copy in sent:
        copy.wait_send()


def local(rows, mods, query_grads, train_grads, token_counts, query_owner, module_map, out_basis, in_basis, eigen_values):
    mine_q = query_grads.shape[0]
    train_rows, slots, feat = train_grads.shape
    columns = feat // LANES
    total_q = rows * mine_q
    tiles = train_rows // TILE
    block = total_q // mods
    staged = train_grads.reshape(train_rows, slots, columns, LANES).transpose(0, 2, 1, 3).reshape(-1, LANES)
    queries = query_grads.reshape(mine_q, slots, columns, LANES).transpose(0, 2, 1, 3).reshape(-1, LANES)
    owner = query_owner[None, :]
    counts = token_counts[None, :]
    vmem = pl.BlockSpec(memory_space=pltpu.VMEM)
    chips = rows // 2
    return pl.pallas_call(
        functools.partial(kernel, rows, mods),
        out_shape=jax.ShapeDtypeStruct((block, train_rows), jnp.float32),
        in_specs=[vmem, pl.BlockSpec(memory_space=pl.ANY), vmem, vmem, pl.BlockSpec(memory_space=pltpu.SMEM), vmem, vmem, vmem],
        out_specs=vmem,
        scratch_shapes=[
            pltpu.VMEM((FACTOR, FACTOR, LANES), jnp.float32),
            pltpu.VMEM((FACTOR, mine_q // HALVES, LANES), jnp.float32),
            pltpu.VMEM((FACTOR, mine_q // HALVES, LANES), jnp.float32),
            pltpu.VMEM((FACTOR, mine_q // HALVES, LANES), jnp.float32),
            pltpu.VMEM((FACTOR, LANES), jnp.float32),
            pltpu.VMEM(staged.shape, jnp.bfloat16),
            pltpu.VMEM((slots, train_rows, feat), jnp.bfloat16),
            pltpu.VMEM((slots, total_q, feat), jnp.bfloat16),
            pltpu.VMEM((total_q // TILE, train_rows, TILE), jnp.float32),
            pltpu.VMEM((tiles, total_q, TILE), jnp.bfloat16),
            pltpu.VMEM((tiles, mods - 1, block, TILE), jnp.bfloat16),
            pltpu.SemaphoreType.DMA((slots,)),
            pltpu.SemaphoreType.DMA((HALVES, slots, max(chips - 1, 1))),
            pltpu.SemaphoreType.DMA((HALVES, slots, chips)),
            pltpu.SemaphoreType.DMA((HALVES, slots, rows)),
            pltpu.SemaphoreType.DMA((tiles, mods - 1)),
            pltpu.SemaphoreType.DMA((tiles, mods - 1)),
        ],
        compiler_params=pltpu.CompilerParams(
            collective_id=0, has_side_effects=True, vmem_limit_bytes=56 * 1024 * 1024
        ),
        name="score",
    )(queries, staged, owner, counts, module_map, out_basis, in_basis, eigen_values)


def solution(mesh):
    in_specs = (
        P(("groups", "rows"), "mods", None),
        P(("groups", "rows"), "mods", None),
        P(("groups", "rows")),
        P("groups"),
        P(),
        P(),
        P(),
        P(),
    )
    out_specs = P(("groups", "mods"), "rows")
    body = functools.partial(local, mesh.shape["rows"], mesh.shape["mods"])
    return jax.shard_map(body, mesh=mesh, in_specs=in_specs, out_specs=out_specs, check_vma=False)
```
